512 devices in a mesh: gx: 4 (over z_hi, core), gy: 16 (over x, y), gz: 8 (over z_lo).
Axes of the slice: x: 4, y: 4, z: 16 (z_hi: 2, z_lo: 8; z = z_hi * 8 + z_lo), core: 2. Of those that a mesh axis runs over, the one named last changes fastest.
Arguments:
- positions: float32 [4, 16, 8, 3, 128], P('gx', 'gy', 'gz'), as said below
- species: int32 [4, 16, 8, 128], P('gx', 'gy', 'gz'), may hold values from 0 to 5
- counts: int32 [4, 16, 8], P('gx', 'gy', 'gz'), may hold values from 64 to 128, as said below
- neighbours: int32 [4, 16, 8, 18, 128], P('gx', 'gy', 'gz'), may hold values from 0 to 1151, as said below
- send_lists: int32 [4, 16, 8, 2, 2, 2, 16], P('gx', 'gy', 'gz'), may hold values from 0 to 127, as said below
- embed: bfloat16 [6, 128], replicated, may hold values from -4 to 4
- radial_in: bfloat16 [2, 8, 64], replicated, may hold values from -6 to 6
- radial_mid: bfloat16 [2, 64, 64], replicated, may hold values from -0.75 to 0.75
- radial_out: bfloat16 [2, 64, 512], replicated, may hold values from -0.75 to 0.75
- up_w: bfloat16 [2, 2, 128, 128], replicated, may hold values from -0.5 to 0.5
- mix_w: bfloat16 [2, 2, 128, 128], replicated, may hold values from -0.5 to 0.5
- out_w: bfloat16 [2, 2, 128, 128], replicated, may hold values from -0.5 to 0.5
- skip_w: bfloat16 [2, 2, 128, 128], replicated, may hold values from -0.5 to 0.5
- product_w: float32 [2, 3, 128], replicated, may hold values from -0.5 to 0.5
- read_one: float32 [128], replicated, may hold values from -0.5 to 0.5
- read_hidden: bfloat16 [128, 16], replicated, may hold values from -0.5 to 0.5
- read_out: float32 [16], replicated, may hold values from -1.5 to 1.5
Outputs:
- energies: float32 [4, 16, 8, 128], P('gx', 'gy', 'gz')
- forces: float32 [4, 16, 8, 3, 128], P('gx', 'gy', 'gz')
- pass_gradient: float32 [4, 16, 8, 4, 128, 128], P('gx', 'gy', 'gz')
The draws below stay inside these ranges and needn't reach their ends.
Inputs may be any that keep to these rules, and one draw needn't show every extreme that they name: `positions`: atom slot a of a brick sits near a lattice site of spacing 3.0 (a different site for each slot), each coordinate within 0.45 of it. `counts`: slots below the count are occupied; some brick has all 128 slots occupied. `neighbours`: each atom lists the 18 sites within 1.5 lattice spacings, occupied or not, as a local slot or as A plus the ghost slot that holds it. `send_lists`: the eight cells together list every slot of the brick exactly once.
All inputs are finite; a program needn't handle non-finite values.
Results may differ from the reference program's by a relative error of at most 0.024.
Values may be sent and summed in bfloat16 or wider, within the bound.
No kernel may reach another device: no remote copies, remote signals or barrier semaphores. Data moves between devices by JAX's collectives and lax.ppermute only.
A program may use at most 128 MiB of HBM per device.

```python
import math
import jax
import jax.numpy as jnp
import numpy as np
from jax import lax

C = 128
H = 64
RHID = 16
S = 6
NRAD = 8
NBR = 18
BLK = 64
LX = 8
LY = 4
LZ = 4
A = 128
G = 16
BX = 4
BY = 16
BZ = 8


def lattice_layout(key):
    bricks = BX * BY * BZ
    keys = jax.random.split(key, bricks)
    return jax.vmap(lambda item: jax.random.permutation(item, A))(keys).astype(jnp.int32)


def inverse_layout(layout):
    counter = jnp.arange(A, dtype=jnp.int32)
    return jax.vmap(lambda row: jnp.zeros((A,), jnp.int32).at[row].set(counter))(layout)


def draw_positions(key, part):
    layout = lattice_layout(key)
    key = jax.random.fold_in(key, 11)
    bricks = BX * BY * BZ
    site_x = layout // (LY * LZ)
    site_y = layout // LZ % LY
    site_z = layout % LZ
    lattice = jnp.stack([site_x, site_y, site_z], 1).astype(jnp.float32) * 3.0
    jitter = jax.random.uniform(key, (bricks, 3, A), jnp.float32, -0.45, 0.45)
    return (lattice + jitter).reshape(BX, BY, BZ, 3, A)


def draw_counts(key, part):
    key = jax.random.fold_in(key, 5)
    bricks = BX * BY * BZ
    key_fill, key_full = jax.random.split(key)
    filled = jax.random.randint(key_fill, (bricks,), A // 2, A + 1, jnp.int32)
    fullest = jax.random.randint(key_full, (), 0, bricks, jnp.int32)
    filled = jnp.where(jnp.arange(bricks, dtype=jnp.int32) == fullest, A, filled)
    return filled.reshape(BX, BY, BZ)


def stencil_offsets():
    found = []
    for step_x in range(-1, 2):
        for step_y in range(-1, 2):
            for step_z in range(-1, 2):
                reach = step_x * step_x + step_y * step_y + step_z * step_z
                if 0 < reach <= 2:
                    found.append((step_x, step_y, step_z))
    return np.array(found, dtype=np.int32)


def draw_neighbours(key, part):
    layout = lattice_layout(key)
    inverse = inverse_layout(layout)
    bricks = BX * BY * BZ
    stencil = jnp.asarray(stencil_offsets())
    half_x = LX // 2
    half_y = LY // 2
    half_z = LZ // 2
    site_x = (layout // (LY * LZ))[:, None, :] + stencil[None, :, 0:1]
    site_y = (layout // LZ % LY)[:, None, :] + stencil[None, :, 1:2]
    site_z = (layout % LZ)[:, None, :] + stencil[None, :, 2:3]
    move_x = jnp.floor_divide(site_x, LX)
    move_y = jnp.floor_divide(site_y, LY)
    move_z = jnp.floor_divide(site_z, LZ)
    wrap_x = site_x - move_x * LX
    wrap_y = site_y - move_y * LY
    wrap_z = site_z - move_z * LZ
    inside = (move_x == 0) & (move_y == 0) & (move_z == 0)
    local_site = (wrap_x * LY + wrap_y) * LZ + wrap_z
    local_slot = jnp.take_along_axis(inverse, local_site.reshape(bricks, -1), axis=1).reshape(local_site.shape)

    def padded(move, wrapped, half):
        return jnp.where(move < 0, 0, jnp.where(move > 0, 3, 1 + wrapped // half))
    rank = (wrap_x % half_x * half_y + wrap_y % half_y) * half_z + wrap_z % half_z
    cell = (padded(move_x, wrap_x, half_x) * 4 + padded(move_y, wrap_y, half_y)) * 4 + padded(move_z, wrap_z, half_z)
    ghost_slot = A + cell * G + rank
    chosen = jnp.where(inside, local_slot, ghost_slot).astype(jnp.int32)
    return chosen.reshape(BX, BY, BZ, NBR, A)


def draw_send_lists(key, part):
    layout = lattice_layout(key)
    inverse = inverse_layout(layout)
    half_x = LX // 2
    half_y = LY // 2
    half_z = LZ // 2
    counter = jnp.arange(8 * G, dtype=jnp.int32)
    cell = counter // G
    rank = counter % G
    cell_x = cell // 4
    cell_y = cell // 2 % 2
    cell_z = cell % 2
    rank_x = rank // (half_y * half_z)
    rank_y = rank // half_z % half_y
    rank_z = rank % half_z
    site = ((cell_x * half_x + rank_x) * LY + cell_y * half_y + rank_y) * LZ + cell_z * half_z + rank_z
    return inverse[:, site].reshape(BX, BY, BZ, 2, 2, 2, G)


def plant(values, stream_key, low, top_value):
    dims = values.shape
    spot = [jax.random.randint(jax.random.fold_in(stream_key, axis), (), 0, dims[axis]) for axis in range(len(dims))]
    values = values.at[tuple(spot)].set(low)
    longest = dims.index(max(dims))
    spot[longest] = (spot[longest] + 1) % dims[longest]
    return values.at[tuple(spot)].set(top_value)


def centred(stream_key, dims, deviation, most, held_as=jnp.bfloat16):
    return jnp.clip(deviation * jax.random.normal(stream_key, dims, jnp.float32), -most, most).astype(held_as)


def setup_inputs(seed: int = 0) -> dict:
    streams_of = jax.random.split(jax.random.key(seed), 18)
    return {
        "positions": draw_positions(jax.random.fold_in(streams_of[17], 71), 0),
        "species": plant(jax.random.randint(streams_of[1], (BX, BY, BZ, A), 0, S), jax.random.fold_in(streams_of[1], 1), 0, S - 1).astype(jnp.int32),
        "counts": draw_counts(jax.random.fold_in(streams_of[17], 71), 0),
        "neighbours": draw_neighbours(jax.random.fold_in(streams_of[17], 71), 0),
        "send_lists": draw_send_lists(jax.random.fold_in(streams_of[17], 71), 0),
        "embed": centred(streams_of[5], (S, C), 1.0, 4.0),
        "radial_in": centred(streams_of[6], (2, NRAD, H), 1 ** -0.5, 6.0),
        "radial_mid": centred(streams_of[7], (2, H, H), H ** -0.5, 0.75),
        "radial_out": centred(streams_of[8], (2, H, 4 * C), H ** -0.5, 0.75),
        "up_w": centred(streams_of[9], (2, 2, C, C), C ** -0.5, 0.5),
        "mix_w": centred(streams_of[10], (2, 2, C, C), C ** -0.5, 0.5),
        "out_w": centred(streams_of[11], (2, 2, C, C), C ** -0.5, 0.5),
        "skip_w": centred(streams_of[12], (2, 2, C, C), C ** -0.5, 0.5),
        "product_w": jnp.clip(jax.random.uniform(streams_of[13], (2, 3, C), jnp.float32, -0.5, 0.5), -0.5, 0.5),
        "read_one": centred(streams_of[14], (C,), C ** -0.5, 0.5, jnp.float32),
        "read_hidden": centred(streams_of[15], (C, RHID), C ** -0.5, 0.5),
        "read_out": centred(streams_of[16], (RHID,), RHID ** -0.5, 1.5, jnp.float32),
    }


RC = 5.0
SPACING = 3.0

def radial_terms(distance):
    orders = jnp.arange(1, NRAD + 1, dtype=jnp.int32).astype(jnp.float32)
    bessel = jnp.sqrt(2.0 / RC) * jnp.sin(orders[:, None] * (jnp.pi / RC) * distance[None, :]) / distance[None, :]
    scaled = jnp.minimum(distance / RC, 1.0)
    envelope = 1.0 - 28.0 * scaled ** 6 + 48.0 * scaled ** 7 - 21.0 * scaled ** 8
    return (bessel, envelope)

def rounded(values):
    narrow = lax.optimization_barrier(values.astype(jnp.bfloat16))
    return values + lax.stop_gradient(narrow.astype(jnp.float32) - values)

def narrowed(values):
    return lax.optimization_barrier(values.astype(jnp.bfloat16)).astype(jnp.float32)

def build_table(own_pos, ghost_pos, ghost_code, species_row, live_count):
    alive = (jnp.arange(A, dtype=jnp.int32) < live_count).astype(jnp.float32)
    codes_own = alive * (species_row.astype(jnp.float32) + 1.0)
    slot_cell = jnp.arange(64 * G, dtype=jnp.int32) // G

    def brick_step(cell_of):
        return (cell_of == 3).astype(jnp.float32) - (cell_of == 0).astype(jnp.float32)
    shifts = jnp.stack([brick_step(slot_cell // 16) * (LX * SPACING), brick_step(slot_cell // 4 % 4) * (LY * SPACING), brick_step(slot_cell % 4) * (LZ * SPACING)])
    table_pos = jnp.concatenate([own_pos, ghost_pos + shifts], 1)
    table_code = jnp.concatenate([codes_own, ghost_code])
    return (table_pos, table_code, alive)

def block_messages(first_atom, own_pos, alive, table_pos, table_live, senders, partners, radial):
    w_first, w_second, w_third = radial
    channels = senders.shape[2]
    with_vectors = senders.shape[0] == 4
    chosen = lax.dynamic_slice_in_dim(partners, first_atom, BLK, 1)
    flat_list = chosen.reshape(-1)
    block_pos = lax.dynamic_slice_in_dim(own_pos, first_atom, BLK, 1)
    block_live = lax.dynamic_slice_in_dim(alive, first_atom, BLK, 0)
    offset_vec = (table_pos[:, flat_list].reshape(3, NBR, BLK) - block_pos[:, None, :]).reshape(3, NBR * BLK)
    distance = jnp.sqrt(lax.optimization_barrier(jnp.sum(offset_vec * offset_vec, axis=0)))
    direction = offset_vec / distance[None, :]
    edge_live = (table_live[flat_list].reshape(NBR, BLK) * block_live[None, :]).reshape(-1)
    bessel, envelope = radial_terms(distance)
    hidden = jax.nn.silu(jnp.dot(bessel.T.astype(jnp.bfloat16), w_first, preferred_element_type=jnp.float32))
    hidden = jax.nn.silu(jnp.dot(hidden.astype(jnp.bfloat16), w_second, preferred_element_type=jnp.float32))
    if with_vectors:
        w_used = w_third
    else:
        w_used = jnp.concatenate([w_third[:, :channels], w_third[:, 2 * channels:3 * channels]], 1)
    weights = jnp.dot(hidden.astype(jnp.bfloat16), w_used, preferred_element_type=jnp.float32)
    weights = (weights * (envelope * edge_live)[:, None]).astype(jnp.bfloat16)
    sender_rows = senders[:, flat_list, :]
    scalar_src = sender_rows[0]
    if with_vectors:
        weight_ss = weights[:, :channels].astype(jnp.float32)
        weight_vs = weights[:, channels:2 * channels].astype(jnp.float32)
        weight_sv = weights[:, 2 * channels:3 * channels].astype(jnp.float32)
        weight_vv = weights[:, 3 * channels:].astype(jnp.float32)
        along = direction[0][:, None] * sender_rows[1] + direction[1][:, None] * sender_rows[2] + direction[2][:, None] * sender_rows[3]
        scalar_msg = weight_ss * scalar_src + weight_vs * along
        vector_msg = weight_sv[None] * scalar_src[None] * direction[:, :, None] + weight_vv[None] * sender_rows[1:]
    else:
        weight_ss = weights[:, :channels].astype(jnp.float32)
        weight_sv = weights[:, channels:].astype(jnp.float32)
        scalar_msg = weight_ss * scalar_src
        vector_msg = weight_sv[None] * scalar_src[None] * direction[:, :, None]
    scalar_sum = scalar_msg.reshape(NBR, BLK, channels).sum(0)
    vector_sum = vector_msg.reshape(3, NBR, BLK, channels).sum(1)
    return jnp.concatenate([scalar_sum[None], vector_sum], 0) / math.sqrt(NBR)

def all_messages(own_pos, alive, table_pos, table_live, senders, partners, radial, live_count, guarded):
    channels = senders.shape[2]

    def one_block(first_atom):
        return block_messages(first_atom, own_pos, alive, table_pos, table_live, senders, partners, radial)
    blocked = jax.checkpoint(one_block)
    if guarded:

        def runner(first_atom):
            return lax.cond(first_atom < live_count, blocked, lambda unused: jnp.zeros((4, BLK, channels), jnp.float32), first_atom)
    else:
        runner = blocked
    starts = jnp.arange(A // BLK, dtype=jnp.int32) * BLK
    stacked = lax.map(runner, starts)
    return jnp.moveaxis(stacked, 0, 1).reshape(4, A, channels)

def node_update(messages, previous, mixing, updating, skipping, products):
    atoms = messages.shape[1]
    channels = messages.shape[2]
    mixed_s = jnp.dot(messages[0].astype(jnp.bfloat16), mixing[0], preferred_element_type=jnp.float32)
    mixed_v = jnp.dot(messages[1:].reshape(3 * atoms, channels).astype(jnp.bfloat16), mixing[1], preferred_element_type=jnp.float32).reshape(3, atoms, channels)
    basis_s = mixed_s + products[0] * mixed_s * mixed_s + products[1] * lax.optimization_barrier(jnp.sum(mixed_v * mixed_v, 0))
    basis_v = mixed_v + products[2] * mixed_s[None] * mixed_v
    new_s = jnp.dot(basis_s.astype(jnp.bfloat16), updating[0], preferred_element_type=jnp.float32)
    new_s = new_s + jnp.dot(previous[0].astype(jnp.bfloat16), skipping[0], preferred_element_type=jnp.float32)
    new_v = jnp.dot(basis_v.reshape(3 * atoms, channels).astype(jnp.bfloat16), updating[1], preferred_element_type=jnp.float32)
    new_v = new_v + jnp.dot(previous[1:].reshape(3 * atoms, channels).astype(jnp.bfloat16), skipping[1], preferred_element_type=jnp.float32)
    return jnp.concatenate([new_s[None], new_v.reshape(3, atoms, channels)], 0)

def layer_one(own_pos, ghost_pos, ghost_code, species_row, live_count, partners, params, guarded):
    embed, radial_in, radial_mid, radial_out, up_w, mix_w, out_w, skip_w, product_w = params[:9]
    table_pos, table_code, alive = build_table(own_pos, ghost_pos, ghost_code, species_row, live_count)
    table_live = (table_code > 0.5).astype(jnp.float32)
    levels = jnp.arange(1, S + 1, dtype=jnp.int32).astype(jnp.float32)
    one_hot = (table_code[:, None] == levels[None, :]).astype(jnp.bfloat16)
    base = jnp.dot(one_hot, embed, preferred_element_type=jnp.float32)
    channels = base.shape[1]
    sender_s = jnp.dot(base.astype(jnp.bfloat16), up_w[0, 0], preferred_element_type=jnp.float32)
    messages = all_messages(own_pos, alive, table_pos, table_live, sender_s[None], partners, (radial_in[0], radial_mid[0], radial_out[0]), live_count, guarded)
    previous = jnp.concatenate([base[None, :A], jnp.zeros((3, A, channels), jnp.float32)], 0)
    features = node_update(messages, previous, mix_w[0], out_w[0], skip_w[0], product_w[0])
    pass_s = jnp.dot(features[0].astype(jnp.bfloat16), up_w[1, 0], preferred_element_type=jnp.float32)
    pass_v = jnp.dot(features[1:].reshape(3 * A, channels).astype(jnp.bfloat16), up_w[1, 1], preferred_element_type=jnp.float32).reshape(3, A, channels)
    passing = rounded(jnp.concatenate([pass_s[None], pass_v], 0))
    return (features, passing)

def layer_two(own_pos, ghost_pos, ghost_code, species_row, live_count, partners, features, passing, ghost_pass, params, guarded):
    embed, radial_in, radial_mid, radial_out, up_w, mix_w, out_w, skip_w, product_w, read_one, read_hidden, read_out = params
    table_pos, table_code, alive = build_table(own_pos, ghost_pos, ghost_code, species_row, live_count)
    table_live = (table_code > 0.5).astype(jnp.float32)
    senders = jnp.concatenate([passing, ghost_pass], 1)
    messages = all_messages(own_pos, alive, table_pos, table_live, senders, partners, (radial_in[1], radial_mid[1], radial_out[1]), live_count, guarded)
    second = node_update(messages, features, mix_w[1], out_w[1], skip_w[1], product_w[1])
    first_energy = lax.optimization_barrier(jnp.sum(features[0] * read_one[None, :], 1))
    hidden = jax.nn.silu(jnp.dot(second[0].astype(jnp.bfloat16), read_hidden, preferred_element_type=jnp.float32))
    second_energy = lax.optimization_barrier(jnp.sum(hidden * read_out[None, :], 1))
    return alive * (first_energy + second_energy)

def expand(buffer, brick_axis, cell_axis):
    lower = jnp.roll(lax.slice_in_dim(buffer, 1, 2, axis=cell_axis), 1, axis=brick_axis)
    upper = jnp.roll(lax.slice_in_dim(buffer, 0, 1, axis=cell_axis), -1, axis=brick_axis)
    return jnp.concatenate([lower, buffer, upper], cell_axis)

def brick_cells(number):
    col_x = number // (BY * BZ)
    col_y = number // BZ % BY
    col_z = number % BZ
    moves = jnp.array([-1, 0, 0, 1], jnp.int32)
    picks = jnp.array([1, 0, 1, 0], jnp.int32)
    return ((col_x + moves) % BX, (col_y + moves) % BY, (col_z + moves) % BZ, picks)

def fetch(grid, number):
    near_x, near_y, near_z, picks = brick_cells(number)
    taken = grid[near_x[:, None, None], near_y[None, :, None], near_z[None, None, :], :, picks[:, None, None], picks[None, :, None], picks[None, None, :]]
    return jnp.moveaxis(taken, 3, 0)

def place(grid, number, values):
    near_x, near_y, near_z, picks = brick_cells(number)
    return grid.at[near_x[:, None, None], near_y[None, :, None], near_z[None, None, :], :, picks[:, None, None], picks[None, :, None], picks[None, None, :]].add(jnp.moveaxis(values, 0, 3))

def reference(positions, species, counts, neighbours, send_lists, embed, radial_in, radial_mid, radial_out, up_w, mix_w, out_w, skip_w, product_w, read_one, read_hidden, read_out):
    params = (embed, radial_in, radial_mid, radial_out, up_w, mix_w, out_w, skip_w, product_w, read_one, read_hidden, read_out)
    bricks = BX * BY * BZ
    channels = embed.shape[1]
    alive = (jnp.arange(A, dtype=jnp.int32)[None, None, None, :] < counts[:, :, :, None]).astype(jnp.float32)
    codes = alive * (species.astype(jnp.float32) + 1.0)
    slots = send_lists.reshape(bricks, 8 * G)
    packed = jnp.concatenate([positions, codes[:, :, :, None, :]], 3).reshape(bricks, 4, A)
    buffer = jax.vmap(lambda rows, chosen: rows[:, chosen])(packed, slots).reshape(BX, BY, BZ, 4, 2, 2, 2, G)
    ghosts = expand(expand(expand(buffer, 0, 4), 1, 5), 2, 6).reshape(bricks, 4, 64 * G)
    pos_all = positions.reshape(bricks, 3, A)
    spec_all = species.reshape(bricks, A)
    count_all = counts.reshape(bricks)
    part_all = neighbours.reshape(bricks, NBR, A)
    numbers = jnp.arange(bricks, dtype=jnp.int32)

    def forward_one(item):
        own_pos, ghost_rows, species_row, live_count, partners = item
        return layer_one(own_pos, ghost_rows[:3], ghost_rows[3], species_row, live_count, partners, params, False)
    features, passing = lax.map(forward_one, (pos_all, ghosts, spec_all, count_all, part_all))
    pass_grid = jax.vmap(lambda rows, chosen: rows[:, chosen, :])(passing, slots).reshape(BX, BY, BZ, 4, 2, 2, 2, G, channels)

    def backward_two(carry, item):
        acc_feat, acc_pos = carry
        number, own_pos, ghost_rows, species_row, live_count, partners, feat_row, pass_row = item
        ghost_pass = fetch(pass_grid, number).reshape(4, 64 * G, channels)

        def local_energy(pos_in, gpos_in, feat_in, pass_in, gpass_in):
            return layer_two(pos_in, gpos_in, ghost_rows[3], species_row, live_count, partners, feat_in, pass_in, gpass_in, params, False)
        energy_row, back = jax.vjp(local_energy, own_pos, ghost_rows[:3], feat_row, pass_row, ghost_pass)
        grad_pos, grad_gpos, grad_feat, grad_pass, grad_gpass = back(jnp.ones_like(energy_row))
        acc_feat = place(acc_feat, number, narrowed(grad_gpass).reshape(4, 4, 4, 4, G, channels))
        acc_pos = place(acc_pos, number, grad_gpos.reshape(3, 4, 4, 4, G))
        return ((acc_feat, acc_pos), (energy_row, grad_pos, grad_feat, grad_pass))
    start = (jnp.zeros((BX, BY, BZ, 4, 2, 2, 2, G, channels), jnp.float32), jnp.zeros((BX, BY, BZ, 3, 2, 2, 2, G), jnp.float32))
    (acc_feat, acc_pos), (energy_all, grad_two, grad_feat, grad_pass) = lax.scan(backward_two, start, (numbers, pos_all, ghosts, spec_all, count_all, part_all, features, passing))
    returned = acc_feat.reshape(bricks, 4, 8 * G, channels)
    grad_pass = jax.vmap(lambda rows, chosen, extra: rows.at[:, chosen, :].add(extra))(grad_pass, slots, returned)

    def backward_one(acc, item):
        number, own_pos, ghost_rows, species_row, live_count, partners, feat_cot, pass_cot = item

        def local_one(pos_in, gpos_in):
            return layer_one(pos_in, gpos_in, ghost_rows[3], species_row, live_count, partners, params, False)
        unused, back = jax.vjp(local_one, own_pos, ghost_rows[:3])
        grad_pos, grad_gpos = back((feat_cot, pass_cot))
        acc = place(acc, number, grad_gpos.reshape(3, 4, 4, 4, G))
        return (acc, grad_pos)
    acc_pos, grad_one = lax.scan(backward_one, acc_pos, (numbers, pos_all, ghosts, spec_all, count_all, part_all, grad_feat, grad_pass))
    summed = grad_one + grad_two
    summed = jax.vmap(lambda rows, chosen, extra: rows.at[:, chosen].add(extra))(summed, slots, acc_pos.reshape(bricks, 3, 8 * G))
    return (energy_all.reshape(BX, BY, BZ, A), (-summed).reshape(BX, BY, BZ, 3, A), grad_pass.reshape(BX, BY, BZ, 4, A, channels))
```

```python
import math

import jax
import jax.numpy as jnp
from jax import lax
from jax.experimental import pallas as pl
from jax.experimental.pallas import tpu as pltpu
from jax.sharding import PartitionSpec as P

NRAD = 8
NBR = 18
A = 128
LX = 8
LY = 4
LZ = 4
RC = 5.0
SPACING = 3.0
C = 128
H = 64

WIDE = 12 * 12 * 16
PLANE = 12 * 16
ROWS1 = 10 * PLANE
TILE = 128
ROWS2 = 8 * TILE
ROWS3 = 6 * TILE
OWN = 4 * 4 * 16
PADR = 32
OFFSETS = [
    (dy, dz, dx)
    for dy in (-1, 0, 1)
    for dz in (-1, 0, 1)
    for dx in (-1, 0, 1)
    if 0 < dy * dy + dz * dz + dx * dx <= 2
]
BF = jnp.bfloat16
F32 = jnp.float32
SCALE = 1.0 / math.sqrt(NBR)
NORM = math.sqrt(2.0 / RC)


def mm(a, b):
    return jnp.dot(a.astype(BF), b.astype(BF), preferred_element_type=F32)


def mm_t(a, b):
    return lax.dot_general(
        a.astype(BF), b.astype(BF), (((1,), (1,)), ((), ())), preferred_element_type=F32
    )


def tmm(a, b):
    return lax.dot_general(
        a.astype(BF), b.astype(BF), (((0,), (0,)), ((), ())), preferred_element_type=F32
    )


def silu(z):
    return 0.5 * z * (1.0 + jnp.tanh(0.5 * z))


def silu_slope(z):
    gate = 0.5 + 0.5 * jnp.tanh(0.5 * z)
    return gate + z * gate * (1.0 - gate)


def sine(turns):
    near = jnp.floor(turns + 0.5)
    part = turns - near
    half = near * 0.5
    odd = (half - jnp.floor(half)) * 2.0
    w = part * math.pi
    q = w * w
    series = 1.0 + q * (
        -1.0 / 6 + q * (1.0 / 120 + q * (-1.0 / 5040 + q * (1.0 / 362880 - q / 39916800)))
    )
    return w * series * (1.0 - 2.0 * odd)


def shape_of(geo):
    d = [geo[k : k + 1] for k in range(3)]
    live = geo[3:4]
    square = d[0] * d[0] + d[1] * d[1] + d[2] * d[2]
    dist = jnp.sqrt(square)
    inv = 1.0 / dist
    u = [x * inv for x in d]
    t = jnp.minimum(dist / RC, 1.0)
    t2 = t * t
    t6 = t2 * t2 * t2
    env = 1.0 - 28.0 * t6 + 48.0 * t6 * t - 21.0 * t6 * t2
    return dist, inv, u, t, env * live, live


def orders(width):
    return (lax.broadcasted_iota(jnp.int32, (NRAD, width), 0) + 1).astype(F32)


def radial_forward(dist, inv, w_in, w_mid):
    k = orders(dist.shape[1])
    bessel = NORM * sine(k * (dist / RC)) * inv
    padded = jnp.concatenate([bessel, jnp.zeros_like(bessel)], 0)
    z1 = mm(w_in, padded)
    z2 = mm(w_mid, silu(z1))
    return bessel, z1, z2


def hidden_stack(h, env, u):
    scaled = h * env
    return jnp.concatenate(
        [scaled.astype(BF)] + [(scaled * u[k]).astype(BF) for k in range(3)], 0
    )


def radial_backward(dist, inv, u, t, env, live, bessel, z1, z2, g, w_mid_fwd, w_in_fwd):
    h = silu(z2)
    parts = [g[k * H : (k + 1) * H] for k in range(4)]
    q = [jnp.sum(h * parts[k], 0, keepdims=True) for k in range(4)]
    gh = env * (parts[0] + u[0] * parts[1] + u[1] * parts[2] + u[2] * parts[3])
    g_env = live * (q[0] + u[0] * q[1] + u[1] * q[2] + u[2] * q[3])
    g_u = [env * q[k + 1] for k in range(3)]
    gz2 = gh * silu_slope(z2)
    gz1 = mm(w_mid_fwd, gz2) * silu_slope(z1)
    gb = mm(w_in_fwd, gz1)[:NRAD]
    k = orders(dist.shape[1])
    slope = (NORM * (k * (math.pi / RC)) * sine(k * (dist / RC) + 0.5) - bessel) * inv
    rest = 1.0 - t
    t2 = t * t
    g_dist = jnp.sum(gb * slope, 0, keepdims=True) + g_env * (
        (-168.0 / RC) * t2 * t2 * t * rest * rest
    )
    along = u[0] * g_u[0] + u[1] * g_u[1] + u[2] * g_u[2]
    return [u[k] * g_dist + (g_u[k] - u[k] * along) * inv for k in range(3)]


def split_mm(perm, x):
    high = x.astype(BF)
    low = (x - high.astype(F32)).astype(BF)
    return jnp.dot(perm, high, preferred_element_type=F32) + jnp.dot(
        perm, low, preferred_element_type=F32
    )


def kernel(
    wide_ref,
    near_ref,
    own_ref,
    perm_ref,
    embed_ref,
    w_in_t_ref,
    w_mid_t_ref,
    w_in_ref,
    w_mid_ref,
    w_out_ref,
    up_ref,
    mix_ref,
    out_ref,
    skip_ref,
    prod_ref,
    read_one_ref,
    read_hidden_ref,
    read_out_ref,
    energy_ref,
    force_ref,
    gpass_ref,
    geo,
    hid,
    send,
    base,
    alv,
    feat,
    pas,
    mixed,
    dm2,
    dfeat,
    dm1,
    gp,
    en,
    wc1,
    wc2,
    geo_own,
    gh1,
    gh2,
    facc,
):
    wc1[...] = jnp.zeros((4 * H, 4 * C), BF)
    wc2[...] = jnp.zeros((4 * H, 8 * C), BF)
    wc1[0:H, 0:C] = w_out_ref[0, :, 0:C]
    wc2[0:H, 0:C] = w_out_ref[1, :, 0:C]
    wc2[0:H, 7 * C : 8 * C] = w_out_ref[1, :, 3 * C : 4 * C]
    for k in range(3):
        rows = slice((k + 1) * H, (k + 2) * H)
        wc1[rows, (k + 1) * C : (k + 2) * C] = w_out_ref[0, :, 2 * C : 3 * C]
        wc2[rows, (k + 1) * C : (k + 2) * C] = w_out_ref[1, :, C : 2 * C]
        wc2[rows, (k + 4) * C : (k + 5) * C] = w_out_ref[1, :, 2 * C : 3 * C]

    wide = wide_ref[...]
    level = lax.broadcasted_iota(jnp.int32, (16, WIDE), 0).astype(F32) + 1.0
    one_hot = (wide[3:4] == level).astype(F32).astype(BF)
    first = tmm(one_hot, embed_ref[...])
    base[...] = first
    alv[...] = tmm(one_hot, jnp.ones((16, C), BF))
    send[0:PADR] = jnp.zeros((PADR, C), F32)
    send[PADR + WIDE : PADR + WIDE + PADR] = jnp.zeros((PADR, C), F32)
    send[PADR : PADR + WIDE] = mm(first, up_ref[0, 0])

    row = lax.broadcasted_iota(jnp.int32, (8, 1), 0)

    def geometry(centre, other):
        alive = (centre > 0.5).astype(F32) * (other > 0.5).astype(F32)
        return jnp.where(row == 3, alive, other - centre)

    def stack_hidden(layer, width):
        w_in = w_in_t_ref[layer]
        w_mid = w_mid_t_ref[layer]

        def one(o, carry):
            dist, inv, u, t, env, live = shape_of(geo[o, :, :width])
            bessel, z1, z2 = radial_forward(dist, inv, w_in, w_mid)
            hid[o, :, :width] = hidden_stack(silu(z2), env, u)
            return carry

        lax.fori_loop(0, NBR, one, 0)

    centre = pltpu.roll(wide, WIDE - PLANE, 1)[:, :ROWS1]
    for o, (dy, dz, dx) in enumerate(OFFSETS):
        shift = PLANE + (dy * 12 + dz) * 16 + dx
        geo[o] = geometry(centre, pltpu.roll(wide, (-shift) % WIDE, 1)[:, :ROWS1])
    stack_hidden(0, ROWS1)

    def rows_one(tile, carry):
        start = pl.multiple_of(tile * TILE, TILE)
        m = [jnp.zeros((TILE, C), F32) for _ in range(4)]
        for o, (dy, dz, dx) in enumerate(OFFSETS):
            w = tmm(hid[o, :, pl.ds(start, TILE)], wc1[...])
            s = send[pl.ds(start + (PADR + PLANE + (dy * 12 + dz) * 16 + dx), TILE), :]
            for c in range(4):
                m[c] = m[c] + w[:, c * C : (c + 1) * C] * s
        prod = prod_ref[0]
        p0, p1, p2 = prod[0:1], prod[1:2], prod[2:3]
        a = [mm(m[c] * SCALE, mix_ref[0, min(c, 1)]) for c in range(4)]
        b_s = a[0] + p0 * a[0] * a[0] + p1 * (a[1] * a[1] + a[2] * a[2] + a[3] * a[3])
        b = [b_s] + [a[c] + p2 * a[0] * a[c] for c in range(1, 4)]
        here = pl.ds(start, TILE)
        for c in range(4):
            new = mm(b[c], out_ref[0, min(c, 1)])
            if c == 0:
                new = new + mm(base[pl.ds(start + PLANE, TILE), :], skip_ref[0, 0])
                feat[here, :] = new
            mixed[c, here, :] = a[c]
            pas[c, here, :] = mm(new, up_ref[1, min(c, 1)]).astype(BF).astype(F32)
        return carry

    lax.fori_loop(0, ROWS1 // TILE, rows_one, 0)

    centre = near_ref[1, :, 2 * TILE : 2 * TILE + ROWS2]
    for o, (dy, dz, dx) in enumerate(OFFSETS):
        shift = 2 * TILE + dy * TILE + dx
        other = pltpu.roll(near_ref[dz + 1], (-shift) % (12 * TILE), 1)[:, :ROWS2]
        geo[o, :, :ROWS2] = geometry(centre, other)
    stack_hidden(1, ROWS2)
    for c in range(4):
        dm2[c, 0:PADR] = jnp.zeros((PADR, C), F32)
        dm2[c, PADR + ROWS2 :] = jnp.zeros((PADR, C), F32)
        dm1[c, 0:PADR] = jnp.zeros((PADR, C), F32)
        dm1[c, PADR + ROWS3 :] = jnp.zeros((PADR, C), F32)

    def rows_two(plane, carry):
        start = pl.multiple_of(plane * TILE, TILE)
        at = pl.multiple_of((plane + 1) * PLANE + 32, 32)
        m = [jnp.zeros((TILE, C), F32) for _ in range(4)]
        for o, (dy, dz, dx) in enumerate(OFFSETS):
            w = tmm(hid[o, :, pl.ds(start, TILE)], wc2[...])
            w = [w[:, c * C : (c + 1) * C] for c in range(8)]
            there = pl.ds(at + ((dy * 12 + dz) * 16 + dx), TILE)
            p = [pas[c, there, :] for c in range(4)]
            m[0] = m[0] + w[0] * p[0] + w[1] * p[1] + w[2] * p[2] + w[3] * p[3]
            for k in range(1, 4):
                m[k] = m[k] + w[k + 3] * p[0] + w[7] * p[k]
        prod = prod_ref[1]
        p0, p1 = prod[0:1], prod[1:2]
        a = [mm(m[c] * SCALE, mix_ref[1, min(c, 1)]) for c in range(4)]
        b_s = a[0] + p0 * a[0] * a[0] + p1 * (a[1] * a[1] + a[2] * a[2] + a[3] * a[3])
        s1 = feat[pl.ds(at, TILE), :]
        s2 = mm(b_s, out_ref[1, 0]) + mm(s1, skip_ref[1, 0])
        zh = mm(s2, read_hidden_ref[...])
        alive = alv[pl.ds(at + PLANE, TILE), :]
        site = jnp.sum(s1 * read_one_ref[...] + silu(zh) * read_out_ref[...], 1, keepdims=True)
        here = pl.ds(start, TILE)
        en[here, :] = alive * site
        gs2 = mm_t(alive * read_out_ref[...] * silu_slope(zh), read_hidden_ref[...])
        gb = mm_t(gs2, out_ref[1, 0])
        dfeat[here, :] = alive * read_one_ref[...] + mm_t(gs2, skip_ref[1, 0])
        inner = pl.ds(start + PADR, TILE)
        dm2[0, inner, :] = mm_t(gb * (1.0 + 2.0 * p0 * a[0]), mix_ref[1, 0]) * SCALE
        for k in range(1, 4):
            dm2[k, inner, :] = mm_t(gb * (2.0 * p1 * a[k]), mix_ref[1, 1]) * SCALE
        return carry

    lax.fori_loop(0, ROWS2 // TILE, rows_two, 0)

    def rows_three(plane, carry):
        start = pl.multiple_of((plane + 1) * TILE, TILE)
        at = pl.multiple_of((plane + 2) * PLANE + 32, 32)
        g = [jnp.zeros((TILE, C), F32) for _ in range(4)]
        for o, (dy, dz, dx) in enumerate(OFFSETS):
            w = tmm(hid[o, :, pl.ds(start, TILE)], wc2[...])
            w = [w[:, c * C : (c + 1) * C] for c in range(8)]
            there = pl.ds(start + (PADR + dy * TILE + dz * 16 + dx), TILE)
            d = [dm2[c, there, :] for c in range(4)]
            g[0] = g[0] + w[0] * d[0] - w[4] * d[1] - w[5] * d[2] - w[6] * d[3]
            for k in range(1, 4):
                g[k] = g[k] - w[k] * d[0] + w[7] * d[k]
        here = pl.ds(pl.multiple_of(plane * TILE, TILE), TILE)
        for c in range(4):
            gp[c, here, :] = g[c]
        f = [mm_t(g[c], up_ref[1, min(c, 1)]) for c in range(4)]
        f[0] = f[0] + dfeat[pl.ds(start, TILE), :]
        b = [mm_t(f[c], out_ref[0, min(c, 1)]) for c in range(4)]
        prod = prod_ref[0]
        p0, p1, p2 = prod[0:1], prod[1:2], prod[2:3]
        a = [mixed[c, pl.ds(at, TILE), :] for c in range(4)]
        ga = [
            b[0] * (1.0 + 2.0 * p0 * a[0]) + p2 * (b[1] * a[1] + b[2] * a[2] + b[3] * a[3])
        ] + [2.0 * b[0] * p1 * a[c] + b[c] * (1.0 + p2 * a[0]) for c in range(1, 4)]
        inner = pl.ds(pl.multiple_of(plane * TILE, TILE) + PADR, TILE)
        for c in range(4):
            dm1[c, inner, :] = mm_t(ga[c], mix_ref[0, min(c, 1)]) * SCALE
        return carry

    lax.fori_loop(0, ROWS3 // TILE, rows_three, 0)

    centre = own_ref[4]
    for o, (dy, dz, dx) in enumerate(OFFSETS):
        other = own_ref[(dy + 1) * 3 + dz + 1]
        if dx != 0:
            other = pltpu.roll(other, (-dx) % OWN, 1)
        geo_own[:, o * OWN : (o + 1) * OWN] = geometry(centre, other)

        one_rows, two_rows = [], []
        for q in range(4):
            i = slice((q + 3) * PLANE + 64, (q + 3) * PLANE + 128)
            j = (q + 3) * PLANE + 64 + (dy * 12 + dz) * 16 + dx
            j = slice(j, j + 64)
            e = PADR + (q + 2) * TILE + 32
            f = e + dy * TILE + dz * 16 + dx
            e, f = slice(e, e + 64), slice(f, f + 64)
            pi = [pas[c, i, :] for c in range(4)]
            pj = [pas[c, j, :] for c in range(4)]
            di = [dm2[c, e, :] for c in range(4)]
            dj = [dm2[c, f, :] for c in range(4)]
            parts = [di[0] * pj[0] + dj[0] * pi[0]]
            parts += [di[0] * pj[k] - dj[0] * pi[k] for k in range(1, 4)]
            parts += [di[k] * pj[0] - dj[k] * pi[0] for k in range(1, 4)]
            last = di[1] * pj[1] + dj[1] * pi[1] + di[2] * pj[2] + dj[2] * pi[2]
            parts += [last + di[3] * pj[3] + dj[3] * pi[3]]
            two_rows.append(jnp.concatenate([x.astype(BF) for x in parts], 1))

            i = PADR + (q + 4) * PLANE + 64
            j = i + (dy * 12 + dz) * 16 + dx
            si, sj = send[i : i + 64, :], send[j : j + 64, :]
            e = PADR + (q + 1) * TILE + 32
            f = e + dy * TILE + dz * 16 + dx
            di = [dm1[c, e : e + 64, :] for c in range(4)]
            dj = [dm1[c, f : f + 64, :] for c in range(4)]
            parts = [di[0] * sj + dj[0] * si]
            parts += [di[k] * sj - dj[k] * si for k in range(1, 4)]
            one_rows.append(jnp.concatenate([x.astype(BF) for x in parts], 1))
        span = slice(o * OWN, (o + 1) * OWN)
        gh1[:, span] = mm_t(wc1[...], jnp.concatenate(one_rows, 0))
        gh2[:, span] = mm_t(wc2[...], jnp.concatenate(two_rows, 0))

    facc[...] = jnp.zeros((8, OWN), F32)

    def own_edges(step, carry):
        span = pl.ds(pl.multiple_of(step * 3 * OWN, TILE), 3 * OWN)
        dist, inv, u, t, env, live = shape_of(geo_own[:, span])
        total = None
        for layer, g in ((0, gh1), (1, gh2)):
            bessel, z1, z2 = radial_forward(
                dist, inv, w_in_t_ref[layer], w_mid_t_ref[layer]
            )
            found = radial_backward(
                dist, inv, u, t, env, live, bessel, z1, z2, g[:, span],
                w_mid_ref[layer], w_in_ref[layer],
            )
            total = found if total is None else [x + y for x, y in zip(total, found)]
        for k in range(3):
            v = total[k]
            facc[k : k + 1, :] += v[:, :OWN] + v[:, OWN : 2 * OWN] + v[:, 2 * OWN :]
        return carry

    lax.fori_loop(0, NBR // 3, own_edges, 0)

    perm = perm_ref[...].astype(BF)
    force = facc[...]
    high = force.astype(BF)
    low = (force - high.astype(F32)).astype(BF)
    force_ref[...] = mm_t(high, perm) + mm_t(low, perm)
    site = jnp.concatenate(
        [en[(q + 2) * TILE + 32 : (q + 2) * TILE + 96, :] for q in range(4)], 0
    )
    energy_ref[...] = split_mm(perm, site)
    for c in range(4):
        own = jnp.concatenate(
            [gp[c, (q + 1) * TILE + 32 : (q + 1) * TILE + 96, :] for q in range(4)], 0
        )
        gpass_ref[c] = split_mm(perm, own)


def compute(wide, near, own, perm, weights, interpret=False):
    scratch = [
        pltpu.VMEM((NBR, 8, ROWS1), F32),
        pltpu.VMEM((NBR, 4 * H, ROWS1), BF),
        pltpu.VMEM((WIDE + 2 * PADR, C), F32),
        pltpu.VMEM((WIDE, C), F32),
        pltpu.VMEM((WIDE, C), F32),
        pltpu.VMEM((ROWS1, C), F32),
        pltpu.VMEM((4, ROWS1, C), F32),
        pltpu.VMEM((4, ROWS1, C), F32),
        pltpu.VMEM((4, ROWS2 + 2 * PADR, C), F32),
        pltpu.VMEM((ROWS2, C), F32),
        pltpu.VMEM((4, ROWS3 + 2 * PADR, C), F32),
        pltpu.VMEM((4, ROWS3, C), F32),
        pltpu.VMEM((ROWS2, C), F32),
        pltpu.VMEM((4 * H, 4 * C), BF),
        pltpu.VMEM((4 * H, 8 * C), BF),
        pltpu.VMEM((8, NBR * OWN), F32),
        pltpu.VMEM((4 * H, NBR * OWN), F32),
        pltpu.VMEM((4 * H, NBR * OWN), F32),
        pltpu.VMEM((8, OWN), F32),
    ]
    return pl.pallas_call(
        kernel,
        out_shape=(
            jax.ShapeDtypeStruct((A, C), F32),
            jax.ShapeDtypeStruct((8, A), F32),
            jax.ShapeDtypeStruct((4, A, C), F32),
        ),
        in_specs=[pl.BlockSpec(memory_space=pltpu.VMEM)] * 18,
        out_specs=[pl.BlockSpec(memory_space=pltpu.VMEM)] * 3,
        scratch_shapes=scratch,
        compiler_params=pltpu.CompilerParams(vmem_limit_bytes=60 * 1024 * 1024),
        interpret=interpret,
    )(wide, near, own, perm, *weights)


def sites_of(pos):
    low = jnp.min(pos, axis=1, keepdims=True)
    step = jnp.floor((pos - low) / SPACING + 0.5).astype(jnp.int32)
    return step[0], step[1], step[2]


def prepare_weights(
    embed, radial_in, radial_mid, radial_out, up_w, mix_w, out_w, skip_w, product_w, read_one,
    read_hidden, read_out,
):
    hidden = read_hidden.shape[1]
    w_in = jnp.pad(radial_in, ((0, 0), (0, 16 - NRAD), (0, 0)))
    return (
        jnp.pad(embed, ((0, 16 - embed.shape[0]), (0, 0))),
        jnp.swapaxes(w_in, 1, 2),
        jnp.swapaxes(radial_mid, 1, 2),
        w_in,
        radial_mid,
        radial_out,
        up_w,
        mix_w,
        out_w,
        skip_w,
        product_w,
        read_one.reshape(1, C),
        jnp.pad(read_hidden, ((0, 0), (0, C - hidden))),
        jnp.pad(read_out, (0, C - hidden)).reshape(1, C),
    )


def windows(wide):
    rows = jnp.pad(wide, ((0, 4), (0, 0), (0, 0), (0, 0)))
    near = jnp.stack([rows[:, :, 2 + d : 10 + d] for d in (-1, 0, 1)]).reshape(3, 8, 12 * TILE)
    own = jnp.stack(
        [rows[:, 4 + e : 8 + e, 4 + d : 8 + d] for e in (-1, 0, 1) for d in (-1, 0, 1)]
    ).reshape(9, 8, OWN)
    return rows.reshape(8, WIDE), near, own


def sort_sites(pos, code):
    x, y, z = sites_of(pos)
    place = (y * LZ + z) * LX + x
    hot = place[:, None] == jnp.arange(A, dtype=jnp.int32)[None, :]
    packed = jnp.concatenate([pos, code[None]], 0)
    ordered = jnp.dot(packed, hot.astype(F32), precision=lax.Precision.HIGHEST)
    wide_place = (y * LZ + z) * 16 + x + 4
    perm = wide_place[:, None] == jnp.arange(OWN, dtype=jnp.int32)[None, :]
    return ordered, perm.astype(F32)


def gather_wide(ordered):
    def three(axis):
        me = lax.axis_index(axis)
        count = lax.axis_size(axis)
        return [(me + count - 1) % count, me, (me + 1) % count]

    columns = lax.axis_size("gx") * lax.axis_size("gz")
    got = lax.all_to_all(
        jnp.broadcast_to(ordered[None], (columns, 4, A)), ("gx", "gz"), 0, 0
    )
    picks = jnp.stack([i * lax.axis_size("gz") + k for i in three("gx") for k in three("gz")])
    got = got[picks].reshape(3, 3, 4, LY, LZ, LX)
    slab = got.transpose(2, 3, 1, 4, 0, 5).reshape(4, LY, 3 * LZ, 3 * LX)[:, :, :, 4:20]

    def moves(size, pad, length):
        at = jnp.arange(size) - pad
        return (at >= length).astype(F32) - (at < 0).astype(F32)

    row = jnp.arange(4)[:, None, None, None]
    step_x = moves(16, 4, LX)[None, None, None, :] * (LX * SPACING)
    step_z = moves(12, 4, LZ)[None, None, :, None] * (LZ * SPACING)
    slab = slab + jnp.where(row == 0, step_x, 0.0) + jnp.where(row == 2, step_z, 0.0)
    count = lax.axis_size("gy")
    forward = [(i, (i + 1) % count) for i in range(count)]
    backward = [(target, source) for source, target in forward]
    flat = slab.reshape(4, LY * PLANE)
    low = lax.ppermute(flat, "gy", forward)
    high = lax.ppermute(flat, "gy", backward)
    row = jnp.arange(4)[:, None]
    move = jnp.where(row == 1, LY * SPACING, 0.0)
    wide = jnp.concatenate([low - move, flat, high + move], 1)
    return wide.reshape(4, 12, 12, 16)


def body(positions, species, counts, neighbours, send_lists, *params):
    pos = positions.reshape(3, A)
    alive = (jnp.arange(A, dtype=jnp.int32) < counts.reshape(())).astype(F32)
    code = alive * (species.reshape(A).astype(F32) + 1.0)
    ordered, perm = sort_sites(pos, code)
    wide = gather_wide(ordered)
    energy, force, grad = compute(*windows(wide), perm, prepare_weights(*params))
    return (
        energy[:, 0].reshape(1, 1, 1, A),
        force[:3].reshape(1, 1, 1, 3, A),
        grad.reshape(1, 1, 1, 4, A, C),
    )


def solution(mesh):
    return jax.shard_map(
        body,
        mesh=mesh,
        in_specs=(
            P("gx", "gy", "gz", None, None),
            P("gx", "gy", "gz", None),
            P("gx", "gy", "gz"),
            P("gx", "gy", "gz", None, None),
            P("gx", "gy", "gz", None, None, None, None),
        )
        + (P(),) * 12,
        out_specs=(
            P("gx", "gy", "gz", None),
            P("gx", "gy", "gz", None, None),
            P("gx", "gy", "gz", None, None, None),
        ),
        check_vma=False,
    )
```

```python
import math

import jax
import jax.numpy as jnp
from jax import lax
from jax.experimental import pallas as pl
from jax.experimental.pallas import tpu as pltpu
from jax.sharding import PartitionSpec as P

NRAD = 8
NBR = 18
A = 128
LX = 8
LY = 4
LZ = 4
RC = 5.0
SPACING = 3.0
C = 128
H = 64

WIDE = 12 * 12 * 16
PLANE = 12 * 16
ROWS1 = 10 * PLANE
TILE = 128
UNROLL = 3
ROWS2 = 8 * TILE
ROWS3 = 6 * TILE
OWN = 4 * 4 * 16
PADR = 32
OFFSETS = [
    (dy, dz, dx)
    for dy in (-1, 0, 1)
    for dz in (-1, 0, 1)
    for dx in (-1, 0, 1)
    if 0 < dy * dy + dz * dz + dx * dx <= 2
]
BF = jnp.bfloat16
F32 = jnp.float32
SCALE = 1.0 / math.sqrt(NBR)
NORM = math.sqrt(2.0 / RC)


def mm(a, b):
    return jnp.dot(a.astype(BF), b.astype(BF), preferred_element_type=F32)


def mm_t(a, b):
    return lax.dot_general(
        a.astype(BF), b.astype(BF), (((1,), (1,)), ((), ())), preferred_element_type=F32
    )


def tmm(a, b):
    return lax.dot_general(
        a.astype(BF), b.astype(BF), (((0,), (0,)), ((), ())), preferred_element_type=F32
    )


def silu(z):
    return 0.5 * z * (1.0 + jnp.tanh(0.5 * z))


def silu_slope(z):
    gate = 0.5 + 0.5 * jnp.tanh(0.5 * z)
    return gate + z * gate * (1.0 - gate)


def silu_of_half(z):
    return z + z * jnp.tanh(z)


def slope_of_half(z):
    gate = 0.5 + 0.5 * jnp.tanh(z)
    return gate + 2.0 * z * gate * (1.0 - gate)


def sine(turns):
    near = jnp.floor(turns + 0.5)
    part = turns - near
    half = near * 0.5
    odd = (half - jnp.floor(half)) * 2.0
    w = part * math.pi
    q = w * w
    series = 1.0 + q * (
        -1.0 / 6 + q * (1.0 / 120 + q * (-1.0 / 5040 + q * (1.0 / 362880 - q / 39916800)))
    )
    return w * series * (1.0 - 2.0 * odd)


def shape_of(geo):
    d = [geo[k : k + 1] for k in range(3)]
    live = geo[3:4]
    square = d[0] * d[0] + d[1] * d[1] + d[2] * d[2]
    dist = jnp.sqrt(square)
    inv = 1.0 / dist
    u = [x * inv for x in d]
    t = jnp.minimum(dist / RC, 1.0)
    t2 = t * t
    t6 = t2 * t2 * t2
    env = 1.0 - 28.0 * t6 + 48.0 * t6 * t - 21.0 * t6 * t2
    return dist, inv, u, t, env * live, live


def orders(width):
    return (lax.broadcasted_iota(jnp.int32, (NRAD, width), 0) + 1).astype(F32)


def radial_forward(dist, inv, w_in, w_mid):
    k = orders(dist.shape[1])
    bessel = NORM * sine(k * (dist / RC)) * inv
    padded = jnp.concatenate([bessel, jnp.zeros_like(bessel)], 0)
    z1 = mm(w_in, padded)
    z2 = mm(w_mid, silu_of_half(z1))
    return bessel, z1, z2


def hidden_stack(h, env, u):
    scaled = h * env
    return jnp.concatenate(
        [scaled.astype(BF)] + [(scaled * u[k]).astype(BF) for k in range(3)], 0
    )


def radial_backward(dist, inv, u, t, env, live, bessel, z1, z2, g, w_mid_fwd, w_in_fwd):
    h = silu_of_half(z2)
    parts = [g[k * H : (k + 1) * H] for k in range(4)]
    q = [jnp.sum(h * parts[k], 0, keepdims=True) for k in range(4)]
    gh = env * (parts[0] + u[0] * parts[1] + u[1] * parts[2] + u[2] * parts[3])
    g_env = live * (q[0] + u[0] * q[1] + u[1] * q[2] + u[2] * q[3])
    g_u = [env * q[k + 1] for k in range(3)]
    gz2 = gh * slope_of_half(z2)
    gz1 = mm(w_mid_fwd, gz2) * slope_of_half(z1)
    gb = mm(w_in_fwd, gz1)[:NRAD]
    k = orders(dist.shape[1])
    slope = (NORM * (k * (math.pi / RC)) * sine(k * (dist / RC) + 0.5) - bessel) * inv
    rest = 1.0 - t
    t2 = t * t
    g_dist = jnp.sum(gb * slope, 0, keepdims=True) + g_env * (
        (-168.0 / RC) * t2 * t2 * t * rest * rest
    )
    along = u[0] * g_u[0] + u[1] * g_u[1] + u[2] * g_u[2]
    return [u[k] * g_dist + (g_u[k] - u[k] * along) * inv for k in range(3)]


def split_mm(perm, x):
    high = x.astype(BF)
    low = (x - high.astype(F32)).astype(BF)
    return jnp.dot(perm, high, preferred_element_type=F32) + jnp.dot(
        perm, low, preferred_element_type=F32
    )


def kernel(
    wide_ref,
    perm_ref,
    embed_ref,
    w_in_t_ref,
    w_mid_t_ref,
    w_in_ref,
    w_mid_ref,
    w_out_ref,
    up_ref,
    mix_ref,
    out_ref,
    skip_ref,
    prod_ref,
    read_one_ref,
    read_hidden_ref,
    read_out_ref,
    energy_ref,
    force_ref,
    gpass_ref,
    geo,
    hid,
    send,
    base,
    alv,
    feat,
    pas,
    mixed,
    dm2,
    dfeat,
    dm1,
    gp,
    en,
    wc1,
    wc2,
    wr,
    near,
    geo_own,
    gh1,
    gh2,
    facc,
):
    wc1[...] = jnp.zeros((4 * H, 4 * C), BF)
    wc2[...] = jnp.zeros((4 * H, 8 * C), BF)
    wc1[0:H, 0:C] = w_out_ref[0, :, 0:C]
    wc2[0:H, 0:C] = w_out_ref[1, :, 0:C]
    wc2[0:H, 7 * C : 8 * C] = w_out_ref[1, :, 3 * C : 4 * C]
    for k in range(3):
        rows = slice((k + 1) * H, (k + 2) * H)
        wc1[rows, (k + 1) * C : (k + 2) * C] = w_out_ref[0, :, 2 * C : 3 * C]
        wc2[rows, (k + 1) * C : (k + 2) * C] = w_out_ref[1, :, C : 2 * C]
        wc2[rows, (k + 4) * C : (k + 5) * C] = w_out_ref[1, :, 2 * C : 3 * C]

    wr[0, :, 0:C] = w_out_ref[1, :, 0:C]
    wr[0, :, C : 2 * C] = w_out_ref[1, :, 3 * C : 4 * C]
    wr[1] = w_out_ref[1, :, C : 3 * C]

    wide = wide_ref[...]
    level = lax.broadcasted_iota(jnp.int32, (16, WIDE), 0).astype(F32) + 1.0
    one_hot = (wide[3:4] == level).astype(F32).astype(BF)
    first = tmm(one_hot, embed_ref[...])
    base[...] = first
    alv[...] = tmm(one_hot, jnp.ones((16, C), BF))
    send[0:PADR] = jnp.zeros((PADR, C), F32)
    send[PADR + WIDE : PADR + WIDE + PADR] = jnp.zeros((PADR, C), F32)
    send[PADR : PADR + WIDE] = mm(first, up_ref[0, 0])

    row = lax.broadcasted_iota(jnp.int32, (8, 1), 0)

    def geometry(centre, other):
        alive = (centre > 0.5).astype(F32) * (other > 0.5).astype(F32)
        return jnp.where(row == 3, alive, other - centre)

    def stack_hidden(layer, width):
        w_in = w_in_t_ref[layer]
        w_mid = w_mid_t_ref[layer]

        def one(o, carry):
            dist, inv, u, t, env, live = shape_of(geo[o, :, :width])
            bessel, z1, z2 = radial_forward(dist, inv, w_in, w_mid)
            hid[o, :, :width] = hidden_stack(silu_of_half(z2), env, u)
            return carry

        lax.fori_loop(0, NBR, one, 0, unroll=UNROLL)

    def edges_two(o, start):
        w = tmm(hid[o, 0:H, pl.ds(start, TILE)], wr[0])
        v = [tmm(hid[o, k * H : (k + 1) * H, pl.ds(start, TILE)], wr[1]) for k in range(1, 4)]
        return [w[:, :C]] + [x[:, :C] for x in v] + [x[:, C:] for x in v] + [w[:, C:]]

    centre = pltpu.roll(wide, WIDE - PLANE, 1)[:, :ROWS1]
    for o, (dy, dz, dx) in enumerate(OFFSETS):
        shift = PLANE + (dy * 12 + dz) * 16 + dx
        geo[o] = geometry(centre, pltpu.roll(wide, (-shift) % WIDE, 1)[:, :ROWS1])
    stack_hidden(0, ROWS1)

    def rows_one(tile, carry):
        start = pl.multiple_of(tile * TILE, TILE)
        m = [jnp.zeros((TILE, C), F32) for _ in range(4)]
        for half in range(2):
            rows, cols = slice(half * C, (half + 1) * C), slice(half * 2 * C, (half + 1) * 2 * C)
            for o, (dy, dz, dx) in enumerate(OFFSETS):
                w = tmm(hid[o, rows, pl.ds(start, TILE)], wc1[rows, cols])
                s = send[pl.ds(start + (PADR + PLANE + (dy * 12 + dz) * 16 + dx), TILE), :]
                m[2 * half] = m[2 * half] + w[:, :C] * s
                m[2 * half + 1] = m[2 * half + 1] + w[:, C:] * s
        prod = prod_ref[0]
        p0, p1, p2 = prod[0:1], prod[1:2], prod[2:3]
        a = [mm(m[c] * SCALE, mix_ref[0, min(c, 1)]) for c in range(4)]
        b_s = a[0] + p0 * a[0] * a[0] + p1 * (a[1] * a[1] + a[2] * a[2] + a[3] * a[3])
        b = [b_s] + [a[c] + p2 * a[0] * a[c] for c in range(1, 4)]
        here = pl.ds(start, TILE)
        for c in range(4):
            new = mm(b[c], out_ref[0, min(c, 1)])
            if c == 0:
                new = new + mm(base[pl.ds(start + PLANE, TILE), :], skip_ref[0, 0])
                feat[here, :] = new
            mixed[c, here, :] = a[c]
            pas[c, here, :] = mm(new, up_ref[1, min(c, 1)]).astype(BF).astype(F32)
        return carry

    lax.fori_loop(0, ROWS1 // TILE, rows_one, 0)

    for d in range(3):
        even = pltpu.roll(wide, WIDE - (1 + d) * 16, 1)
        odd = pltpu.roll(wide, WIDE - (1 + d) * 16 - 64, 1)
        for y in range(12):
            at = y * PLANE - y % 2 * 64
            near[d, :, y * TILE : (y + 1) * TILE] = (odd if y % 2 else even)[:, at : at + TILE]
    centre = near[1, :, 2 * TILE : 2 * TILE + ROWS2]
    for o, (dy, dz, dx) in enumerate(OFFSETS):
        shift = 2 * TILE + dy * TILE + dx
        other = pltpu.roll(near[dz + 1], (-shift) % (12 * TILE), 1)[:, :ROWS2]
        geo[o, :, :ROWS2] = geometry(centre, other)
    stack_hidden(1, ROWS2)
    for c in range(4):
        dm2[c, 0:PADR] = jnp.zeros((PADR, C), F32)
        dm2[c, PADR + ROWS2 :] = jnp.zeros((PADR, C), F32)
        dm1[c, 0:PADR] = jnp.zeros((PADR, C), F32)
        dm1[c, PADR + ROWS3 :] = jnp.zeros((PADR, C), F32)

    def rows_two(plane, carry):
        start = pl.multiple_of(plane * TILE, TILE)
        at = pl.multiple_of((plane + 1) * PLANE + 32, 32)
        m = [jnp.zeros((TILE, C), F32) for _ in range(4)]
        for o, (dy, dz, dx) in enumerate(OFFSETS):
            w = edges_two(o, start)
            there = pl.ds(at + ((dy * 12 + dz) * 16 + dx), TILE)
            p = [pas[c, there, :] for c in range(4)]
            m[0] = m[0] + w[0] * p[0] + w[1] * p[1] + w[2] * p[2] + w[3] * p[3]
            for k in range(1, 4):
                m[k] = m[k] + w[k + 3] * p[0] + w[7] * p[k]
        prod = prod_ref[1]
        p0, p1 = prod[0:1], prod[1:2]
        a = [mm(m[c] * SCALE, mix_ref[1, min(c, 1)]) for c in range(4)]
        b_s = a[0] + p0 * a[0] * a[0] + p1 * (a[1] * a[1] + a[2] * a[2] + a[3] * a[3])
        s1 = feat[pl.ds(at, TILE), :]
        s2 = mm(b_s, out_ref[1, 0]) + mm(s1, skip_ref[1, 0])
        zh = mm(s2, read_hidden_ref[...])
        alive = alv[pl.ds(at + PLANE, TILE), :]
        site = jnp.sum(s1 * read_one_ref[...] + silu(zh) * read_out_ref[...], 1, keepdims=True)
        here = pl.ds(start, TILE)
        en[here, :] = alive * site
        gs2 = mm_t(alive * read_out_ref[...] * silu_slope(zh), read_hidden_ref[...])
        gb = mm_t(gs2, out_ref[1, 0])
        dfeat[here, :] = alive * read_one_ref[...] + mm_t(gs2, skip_ref[1, 0])
        inner = pl.ds(start + PADR, TILE)
        dm2[0, inner, :] = mm_t(gb * (1.0 + 2.0 * p0 * a[0]), mix_ref[1, 0]) * SCALE
        for k in range(1, 4):
            dm2[k, inner, :] = mm_t(gb * (2.0 * p1 * a[k]), mix_ref[1, 1]) * SCALE
        return carry

    lax.fori_loop(0, ROWS2 // TILE, rows_two, 0)

    def rows_three(plane, carry):
        start = pl.multiple_of((plane + 1) * TILE, TILE)
        at = pl.multiple_of((plane + 2) * PLANE + 32, 32)
        g = [jnp.zeros((TILE, C), F32) for _ in range(4)]
        for o, (dy, dz, dx) in enumerate(OFFSETS):
            w = edges_two(o, start)
            there = pl.ds(start + (PADR + dy * TILE + dz * 16 + dx), TILE)
            d = [dm2[c, there, :] for c in range(4)]
            g[0] = g[0] + w[0] * d[0] - w[4] * d[1] - w[5] * d[2] - w[6] * d[3]
            for k in range(1, 4):
                g[k] = g[k] - w[k] * d[0] + w[7] * d[k]
        here = pl.ds(pl.multiple_of(plane * TILE, TILE), TILE)
        for c in range(4):
            gp[c, here, :] = g[c]
        f = [mm_t(g[c], up_ref[1, min(c, 1)]) for c in range(4)]
        f[0] = f[0] + dfeat[pl.ds(start, TILE), :]
        b = [mm_t(f[c], out_ref[0, min(c, 1)]) for c in range(4)]
        prod = prod_ref[0]
        p0, p1, p2 = prod[0:1], prod[1:2], prod[2:3]
        a = [mixed[c, pl.ds(at, TILE), :] for c in range(4)]
        ga = [
            b[0] * (1.0 + 2.0 * p0 * a[0]) + p2 * (b[1] * a[1] + b[2] * a[2] + b[3] * a[3])
        ] + [2.0 * b[0] * p1 * a[c] + b[c] * (1.0 + p2 * a[0]) for c in range(1, 4)]
        inner = pl.ds(pl.multiple_of(plane * TILE, TILE) + PADR, TILE)
        for c in range(4):
            dm1[c, inner, :] = mm_t(ga[c], mix_ref[0, min(c, 1)]) * SCALE
        return carry

    lax.fori_loop(0, ROWS3 // TILE, rows_three, 0)

    first_half = lax.broadcasted_iota(jnp.int32, (8, TILE), 1) < 64

    def own_window(dy, dz):
        low = pltpu.roll(near[dz + 1], 12 * TILE - 32, 1)
        high = pltpu.roll(near[dz + 1], 32, 1)
        found = []
        for q in (0, 2):
            at = (4 + dy + q) * TILE
            found.append(
                jnp.where(first_half, low[:, at : at + TILE], high[:, at + TILE : at + 2 * TILE])
            )
        return jnp.concatenate(found, 1)

    centre = own_window(0, 0)
    for o, (dy, dz, dx) in enumerate(OFFSETS):
        other = own_window(dy, dz)
        if dx != 0:
            other = pltpu.roll(other, (-dx) % OWN, 1)
        geo_own[:, o * OWN : (o + 1) * OWN] = geometry(centre, other)

        one_rows, two_rows = [], []
        for q in range(4):
            i = slice((q + 3) * PLANE + 64, (q + 3) * PLANE + 128)
            j = (q + 3) * PLANE + 64 + (dy * 12 + dz) * 16 + dx
            j = slice(j, j + 64)
            e = PADR + (q + 2) * TILE + 32
            f = e + dy * TILE + dz * 16 + dx
            e, f = slice(e, e + 64), slice(f, f + 64)
            pi = [pas[c, i, :] for c in range(4)]
            pj = [pas[c, j, :] for c in range(4)]
            di = [dm2[c, e, :] for c in range(4)]
            dj = [dm2[c, f, :] for c in range(4)]
            parts = [di[0] * pj[0] + dj[0] * pi[0]]
            parts += [di[0] * pj[k] - dj[0] * pi[k] for k in range(1, 4)]
            parts += [di[k] * pj[0] - dj[k] * pi[0] for k in range(1, 4)]
            last = di[1] * pj[1] + dj[1] * pi[1] + di[2] * pj[2] + dj[2] * pi[2]
            parts += [last + di[3] * pj[3] + dj[3] * pi[3]]
            two_rows.append(jnp.concatenate([x.astype(BF) for x in parts], 1))

            i = PADR + (q + 4) * PLANE + 64
            j = i + (dy * 12 + dz) * 16 + dx
            si, sj = send[i : i + 64, :], send[j : j + 64, :]
            e = PADR + (q + 1) * TILE + 32
            f = e + dy * TILE + dz * 16 + dx
            di = [dm1[c, e : e + 64, :] for c in range(4)]
            dj = [dm1[c, f : f + 64, :] for c in range(4)]
            parts = [di[0] * sj + dj[0] * si]
            parts += [di[k] * sj - dj[k] * si for k in range(1, 4)]
            one_rows.append(jnp.concatenate([x.astype(BF) for x in parts], 1))
        span = slice(o * OWN, (o + 1) * OWN)
        gh1[:, span] = mm_t(wc1[...], jnp.concatenate(one_rows, 0))
        gh2[:, span] = mm_t(wc2[...], jnp.concatenate(two_rows, 0))

    facc[...] = jnp.zeros((8, OWN), F32)

    def own_edges(step, carry):
        span = pl.ds(pl.multiple_of(step * 3 * OWN, TILE), 3 * OWN)
        dist, inv, u, t, env, live = shape_of(geo_own[:, span])
        total = None
        for layer, g in ((0, gh1), (1, gh2)):
            bessel, z1, z2 = radial_forward(
                dist, inv, w_in_t_ref[layer], w_mid_t_ref[layer]
            )
            found = radial_backward(
                dist, inv, u, t, env, live, bessel, z1, z2, g[:, span],
                w_mid_ref[layer], w_in_ref[layer],
            )
            total = found if total is None else [x + y for x, y in zip(total, found)]
        for k in range(3):
            v = total[k]
            facc[k : k + 1, :] += v[:, :OWN] + v[:, OWN : 2 * OWN] + v[:, 2 * OWN :]
        return carry

    lax.fori_loop(0, NBR // 3, own_edges, 0)

    perm = perm_ref[...].astype(BF)
    force = facc[...]
    high = force.astype(BF)
    low = (force - high.astype(F32)).astype(BF)
    force_ref[...] = mm_t(high, perm) + mm_t(low, perm)
    site = jnp.concatenate(
        [en[(q + 2) * TILE + 32 : (q + 2) * TILE + 96, :] for q in range(4)], 0
    )
    energy_ref[...] = split_mm(perm, site)
    for c in range(4):
        own = jnp.concatenate(
            [gp[c, (q + 1) * TILE + 32 : (q + 1) * TILE + 96, :] for q in range(4)], 0
        )
        gpass_ref[c] = split_mm(perm, own)


def compute(wide, perm, weights, interpret=False):
    scratch = [
        pltpu.VMEM((NBR, 8, ROWS1), F32),
        pltpu.VMEM((NBR, 4 * H, ROWS1), BF),
        pltpu.VMEM((WIDE + 2 * PADR, C), F32),
        pltpu.VMEM((WIDE, C), F32),
        pltpu.VMEM((WIDE, C), F32),
        pltpu.VMEM((ROWS1, C), F32),
        pltpu.VMEM((4, ROWS1, C), F32),
        pltpu.VMEM((4, ROWS1, C), F32),
        pltpu.VMEM((4, ROWS2 + 2 * PADR, C), F32),
        pltpu.VMEM((ROWS2, C), F32),
        pltpu.VMEM((4, ROWS3 + 2 * PADR, C), F32),
        pltpu.VMEM((4, ROWS3, C), F32),
        pltpu.VMEM((ROWS2, C), F32),
        pltpu.VMEM((4 * H, 4 * C), BF),
        pltpu.VMEM((4 * H, 8 * C), BF),
        pltpu.VMEM((2, H, 2 * C), BF),
        pltpu.VMEM((3, 8, 12 * TILE), F32),
        pltpu.VMEM((8, NBR * OWN), F32),
        pltpu.VMEM((4 * H, NBR * OWN), F32),
        pltpu.VMEM((4 * H, NBR * OWN), F32),
        pltpu.VMEM((8, OWN), F32),
    ]
    return pl.pallas_call(
        kernel,
        out_shape=(
            jax.ShapeDtypeStruct((A, C), F32),
            jax.ShapeDtypeStruct((8, A), F32),
            jax.ShapeDtypeStruct((4, A, C), F32),
        ),
        in_specs=[pl.BlockSpec(memory_space=pltpu.VMEM)] * 16,
        out_specs=[pl.BlockSpec(memory_space=pltpu.VMEM)] * 3,
        scratch_shapes=scratch,
        compiler_params=pltpu.CompilerParams(vmem_limit_bytes=60 * 1024 * 1024),
        interpret=interpret,
    )(wide, perm, *weights)


def sites_of(pos):
    low = jnp.min(pos, axis=1, keepdims=True)
    step = jnp.floor((pos - low) / SPACING + 0.5).astype(jnp.int32)
    return step[0], step[1], step[2]


def prepare_weights(
    embed, radial_in, radial_mid, radial_out, up_w, mix_w, out_w, skip_w, product_w, read_one,
    read_hidden, read_out,
):
    hidden = read_hidden.shape[1]
    half = jnp.asarray(0.5, BF)
    w_in = jnp.pad(radial_in, ((0, 0), (0, 16 - NRAD), (0, 0)))
    return (
        jnp.pad(embed, ((0, 16 - embed.shape[0]), (0, 0))),
        jnp.swapaxes(w_in, 1, 2) * half,
        jnp.swapaxes(radial_mid, 1, 2) * half,
        w_in,
        radial_mid,
        radial_out,
        up_w,
        mix_w,
        out_w,
        skip_w,
        product_w,
        read_one.reshape(1, C),
        jnp.pad(read_hidden, ((0, 0), (0, C - hidden))),
        jnp.pad(read_out, (0, C - hidden)).reshape(1, C),
    )


def sort_sites(pos, code):
    x, y, z = sites_of(pos)
    place = (y * LZ + z) * LX + x
    hot = place[:, None] == jnp.arange(A, dtype=jnp.int32)[None, :]
    packed = jnp.concatenate([pos, code[None]], 0)
    ordered = jnp.dot(packed, hot.astype(F32), precision=lax.Precision.HIGHEST)
    wide_place = (y * LZ + z) * 16 + x + 4
    perm = wide_place[:, None] == jnp.arange(OWN, dtype=jnp.int32)[None, :]
    return ordered, perm.astype(F32)


def gather_wide(ordered):
    def three(axis):
        me = lax.axis_index(axis)
        count = lax.axis_size(axis)
        return [(me + count - 1) % count, me, (me + 1) % count]

    columns = lax.axis_size("gx") * lax.axis_size("gz")
    got = lax.all_to_all(
        jnp.broadcast_to(ordered[None], (columns, 4, A)), ("gx", "gz"), 0, 0
    )
    picks = jnp.stack([i * lax.axis_size("gz") + k for i in three("gx") for k in three("gz")])
    got = got[picks].reshape(3, 3, 4, LY, LZ, LX)
    slab = got.transpose(2, 3, 1, 4, 0, 5).reshape(4, LY, 3 * LZ, 3 * LX)[:, :, :, 4:20]

    def moves(size, pad, length):
        at = jnp.arange(size) - pad
        return (at >= length).astype(F32) - (at < 0).astype(F32)

    row = jnp.arange(4)[:, None, None, None]
    step_x = moves(16, 4, LX)[None, None, None, :] * (LX * SPACING)
    step_z = moves(12, 4, LZ)[None, None, :, None] * (LZ * SPACING)
    slab = slab + jnp.where(row == 0, step_x, 0.0) + jnp.where(row == 2, step_z, 0.0)
    count = lax.axis_size("gy")
    forward = [(i, (i + 1) % count) for i in range(count)]
    backward = [(target, source) for source, target in forward]
    flat = slab.reshape(4, LY * PLANE)
    low = lax.ppermute(flat, "gy", forward)
    high = lax.ppermute(flat, "gy", backward)
    row = jnp.arange(4)[:, None]
    move = jnp.where(row == 1, LY * SPACING, 0.0)
    wide = jnp.concatenate([low - move, flat, high + move], 1)
    return jnp.pad(wide, ((0, 4), (0, 0)))


def body(positions, species, counts, neighbours, send_lists, *params):
    pos = positions.reshape(3, A)
    alive = (jnp.arange(A, dtype=jnp.int32) < counts.reshape(())).astype(F32)
    code = alive * (species.reshape(A).astype(F32) + 1.0)
    ordered, perm = sort_sites(pos, code)
    wide = gather_wide(ordered)
    energy, force, grad = compute(wide, perm, prepare_weights(*params))
    return (
        energy[:, 0].reshape(1, 1, 1, A),
        force[:3].reshape(1, 1, 1, 3, A),
        grad.reshape(1, 1, 1, 4, A, C),
    )


def solution(mesh):
    return jax.shard_map(
        body,
        mesh=mesh,
        in_specs=(
            P("gx", "gy", "gz", None, None),
            P("gx", "gy", "gz", None),
            P("gx", "gy", "gz"),
            P("gx", "gy", "gz", None, None),
            P("gx", "gy", "gz", None, None, None, None),
        )
        + (P(),) * 12,
        out_specs=(
            P("gx", "gy", "gz", None),
            P("gx", "gy", "gz", None, None),
            P("gx", "gy", "gz", None, None, None),
        ),
        check_vma=False,
    )
```
